32 devices in a mesh: row: 4 (over x, core), col: 8 (over z, y).
Axes of the slice: x: 2, y: 2, z: 4, core: 2. Of those that a mesh axis runs over, the one named last changes fastest.
Arguments:
- features: bfloat16 [8, 4, 128, 256], P('col', 'row'), may hold values from -6 to 6
- weight: bfloat16 [256, 256], replicated, may hold values from -0.375 to 0.375
- out_bias: float32 [256], replicated, may hold values from -3 to 3
- tile_values: bfloat16 [4, 8, 8, 3, 128, 128], P('row', 'col'), may hold values from -0.109375 to 0.109375
- tile_cols: int32 [4, 8, 8, 3], P('row', 'col'), may hold values from 0 to 3, as said below
- tile_counts: int32 [4, 8, 8], P('row', 'col'), may hold values from 1 to 3, as said below
- cotangent: bfloat16 [4, 8, 128, 256], P('row', 'col'), may hold values from -6 to 6
Outputs:
- activated: bfloat16 [4, 8, 128, 256], P('row', 'col')
- feature_grad: bfloat16 [8, 4, 128, 256], P('col', 'row')
The draws below stay inside these ranges and needn't reach their ends.
Inputs may be any that keep to these rules, and one draw needn't show every extreme that they name: `tile_cols`: the 3 column tile numbers of one row tile are distinct. `tile_counts`: in every device's block some row tile has all 3 slots live; slots at or past a row tile's count are unused.
All inputs are finite; a program needn't handle non-finite values.
Results may differ from the reference program's by a relative error of at most 0.03.
Values may be sent and summed in bfloat16 or wider, within the bound.
No kernel may reach another device: no remote copies, remote signals or barrier semaphores. Data moves between devices by JAX's collectives and lax.ppermute only.
A program may use at most 64 MiB of HBM per device.

```python
import jax
import jax.numpy as jnp
from jax import lax

F = 256
TILE = 128
K = 3
SUB = 128
NODES = 4096
ROW_TILES = 8
COL_TILES = 4
N_ROW = 4
N_COL = 8


def draw_tile_cols(key, part):
    key = jax.random.fold_in(key, 11)
    raw_bits = jax.random.randint(key, (N_ROW, N_COL, ROW_TILES, COL_TILES), 0, 1 << 20)
    scores = raw_bits * COL_TILES + jnp.arange(COL_TILES, dtype=jnp.int32)
    ordering = jnp.argsort(scores, axis=-1, stable=True)
    return ordering[..., :K].astype(jnp.int32)


def draw_tile_counts(key, part):
    key = jax.random.fold_in(key, 12)
    key_floor, key_rows, key_full = jax.random.split(key, 3)
    floor_level = jax.random.randint(key_floor, (N_ROW, N_COL, 1), 1, K + 1)
    raw_bits = jax.random.randint(key_rows, (N_ROW, N_COL, ROW_TILES), 0, 1 << 20)
    counts = floor_level + raw_bits % (K + 1 - floor_level)
    full_at = jax.random.randint(key_full, (N_ROW, N_COL, 1), 0, ROW_TILES)
    row_ids = jnp.arange(ROW_TILES, dtype=jnp.int32)[None, None, :]
    return jnp.where(row_ids == full_at, K, counts).astype(jnp.int32)


def shard_levels(own_key, shape, cuts, least, top_value):
    factor_of = 1.0
    for position, blocks in cuts:
        heights = jax.random.uniform(jax.random.fold_in(jax.random.fold_in(own_key, 6), position), (blocks,), jnp.float32, least / len(cuts), top_value / len(cuts))
        factor_of = factor_of * jnp.repeat(jnp.exp(heights), shape[position] // blocks).reshape((-1,) + (1,) * (len(shape) - 1 - position))
    return factor_of


def bell_draw(own_key, shape, width, most, shards=(), held_as=jnp.bfloat16):
    drawn = jax.random.normal(own_key, shape, jnp.float32) * width
    if len(shards) > 0:
        drawn = shard_levels(own_key, shape, shards, -0.22, 0.18) * drawn
    return jnp.clip(drawn, min=-most, max=most).astype(held_as)


def setup_inputs(seed: int = 0) -> dict:
    seeds = jax.random.split(jax.random.key(seed), 8)
    return {
        "features": bell_draw(seeds[0], (N_COL, N_ROW, SUB, F), 1.0, 6.0, ((0, 8), (1, 4))),
        "weight": bell_draw(seeds[1], (F, F), F ** -0.5, 0.375),
        "out_bias": bell_draw(seeds[2], (F,), 0.5, 3.0, (), jnp.float32),
        "tile_values": bell_draw(seeds[3], (N_ROW, N_COL, ROW_TILES, K, TILE, TILE), (TILE * K * N_COL) ** -0.5, 0.109375, ((0, 4), (1, 8))),
        "tile_cols": draw_tile_cols(jax.random.fold_in(seeds[7], 71), 0),
        "tile_counts": draw_tile_counts(jax.random.fold_in(seeds[7], 71), 0),
        "cotangent": bell_draw(seeds[6], (N_ROW, N_COL, SUB, F), 1.0, 6.0, ((0, 4), (1, 8))),
    }


def masked_tiles(tile_values, tile_counts, row_idx, col_idx):
    slot_ids = jnp.arange(K, dtype=jnp.int32)
    live = (slot_ids[None, :] < tile_counts[row_idx, col_idx][:, None]).astype(jnp.float32)
    return tile_values[row_idx, col_idx].astype(jnp.float32) * live[:, :, None, None]


def rounded(value):
    return lax.optimization_barrier(value.astype(jnp.bfloat16)).astype(jnp.float32)


def reference(features, weight, out_bias, tile_values, tile_cols, tile_counts, cotangent):
    flat_feats = features.reshape(NODES, F)
    projected = jnp.dot(flat_feats, weight, preferred_element_type=jnp.float32).astype(jnp.bfloat16)
    panels = projected.reshape(N_COL, COL_TILES, TILE, F)

    def forward_row(row_idx):
        def step(running, col_idx):
            tile_set = masked_tiles(tile_values, tile_counts, row_idx, col_idx)
            gathered = panels[col_idx][tile_cols[row_idx, col_idx]].astype(jnp.float32)
            partial_value = jnp.einsum("tkij,tkjf->tif", tile_set, gathered, precision=lax.Precision.HIGHEST)
            return running + rounded(partial_value), None
        running, _ = lax.scan(step, jnp.zeros((ROW_TILES, TILE, F), jnp.float32), jnp.arange(N_COL, dtype=jnp.int32))
        return running.reshape(ROW_TILES * TILE, F)

    preact = lax.map(forward_row, jnp.arange(N_ROW, dtype=jnp.int32)) + out_bias
    sigmoid_z = jax.nn.sigmoid(preact)
    activated = (preact * sigmoid_z).astype(jnp.bfloat16).reshape(N_ROW, N_COL, SUB, F)
    slope = sigmoid_z * (1.0 + preact * (1.0 - sigmoid_z))
    pre_grad = (cotangent.reshape(N_ROW, SUB * N_COL, F).astype(jnp.float32) * slope).astype(jnp.bfloat16)
    grad_tiles = pre_grad.reshape(N_ROW, ROW_TILES, TILE, F)
    col_ids = jnp.arange(COL_TILES, dtype=jnp.int32)

    def backward_col(col_idx):
        def step(running, row_idx):
            tile_set = masked_tiles(tile_values, tile_counts, row_idx, col_idx)
            contrib = jnp.einsum("tkij,tif->tkjf", tile_set, grad_tiles[row_idx].astype(jnp.float32), precision=lax.Precision.HIGHEST)
            selector = (tile_cols[row_idx, col_idx][:, :, None] == col_ids[None, None, :]).astype(jnp.float32)
            partial_value = jnp.einsum("tkc,tkjf->cjf", selector, contrib, precision=lax.Precision.HIGHEST)
            return running + rounded(partial_value), None
        running, _ = lax.scan(step, jnp.zeros((COL_TILES, TILE, F), jnp.float32), jnp.arange(N_ROW, dtype=jnp.int32))
        return running

    spread = lax.map(backward_col, jnp.arange(N_COL, dtype=jnp.int32)).astype(jnp.bfloat16).reshape(NODES, F)
    feature_grad = jnp.dot(spread, weight.T, preferred_element_type=jnp.float32).astype(jnp.bfloat16)
    return activated, feature_grad.reshape(N_COL, N_ROW, SUB, F)
```

```python
import jax
import jax.numpy as jnp
from jax import lax
from jax.sharding import PartitionSpec as P


def silu_slope(preact):
    sigmoid_z = jax.nn.sigmoid(preact)
    return (preact * sigmoid_z, sigmoid_z * (1.0 + preact * (1.0 - sigmoid_z)))


def shift(value, axis, step):
    size = lax.axis_size(axis)
    return lax.ppermute(value, axis, [(i, (i + step) % size) for i in range(size)])


def gather_all(value, axis):
    size = lax.axis_size(axis)
    me = lax.axis_index(axis)
    parts = [value] + [shift(value, axis, -step) for step in range(1, size)]
    stacked = jnp.stack(parts)
    return stacked[(jnp.arange(size) - me) % size]


def scatter_sum(value, axis):
    size = lax.axis_size(axis)
    me = lax.axis_index(axis)
    total = lax.dynamic_index_in_dim(value, me, 0, False).astype(jnp.float32)
    for step in range(1, size):
        part = lax.dynamic_index_in_dim(value, (me + step) % size, 0, False)
        total = total + shift(part, axis, step).astype(jnp.float32)
    return total


def shards(features, weight, out_bias, tile_values, tile_cols, tile_counts, cotangent):
    tile_size = tile_values.shape[-1]
    width = weight.shape[1]
    slot_count = tile_values.shape[3]
    row_tiles = tile_values.shape[2]
    slot_ids = jnp.arange(slot_count, dtype=jnp.int32)
    live = (slot_ids[None, :] < tile_counts[0, 0][:, None]).astype(jnp.bfloat16)
    tile_set = tile_values[0, 0] * live[:, :, None, None]
    col_index = tile_cols[0, 0]
    projected = jnp.dot(features[0, 0], weight, preferred_element_type=jnp.float32).astype(
        jnp.bfloat16
    )
    panel = lax.all_gather(projected, "row", axis=0)
    col_tiles = panel.shape[0]
    gathered = panel[col_index]
    product = jnp.einsum("tkij,tkjf->tif", tile_set, gathered, preferred_element_type=jnp.float32)
    preact = scatter_sum(product.astype(jnp.bfloat16), "col") + out_bias
    activated, slope = silu_slope(preact)
    pre_grad = (cotangent[0, 0].astype(jnp.float32) * slope).astype(jnp.bfloat16)
    grad_tiles = gather_all(pre_grad, "col")
    back_terms = jnp.zeros((col_tiles, tile_size, width), jnp.float32)
    for slot in range(slot_count):
        contrib = jnp.einsum(
            "tij,tif->tjf", tile_set[:, slot], grad_tiles, preferred_element_type=jnp.float32
        )
        back_terms = back_terms + jax.ops.segment_sum(
            contrib, col_index[:, slot], num_segments=col_tiles
        )
    spread = scatter_sum(back_terms.astype(jnp.bfloat16), "row").astype(jnp.bfloat16)
    feature_grad = jnp.dot(spread, weight.T, preferred_element_type=jnp.float32)
    return (
        activated.astype(jnp.bfloat16)[None, None],
        feature_grad.astype(jnp.bfloat16)[None, None],
    )


def solution(mesh):
    in_specs = (
        P("col", "row", None, None),
        P(),
        P(),
        P("row", "col", None, None, None, None),
        P("row", "col", None, None),
        P("row", "col", None),
        P("row", "col", None, None),
    )
    out_specs = (P("row", "col", None, None), P("col", "row", None, None))
    return jax.shard_map(shards, mesh=mesh, in_specs=in_specs, out_specs=out_specs, check_vma=False)
```

```python
import jax
import jax.numpy as jnp
from jax import lax
from jax.experimental import pallas as pl
from jax.experimental.pallas import tpu as pltpu
from jax.sharding import PartitionSpec as P

BOTH = ("row", "col")
HBM = pl.BlockSpec(memory_space=pltpu.HBM)


def silu_slope(preact):
    sigmoid_z = jax.nn.sigmoid(preact)
    return (preact * sigmoid_z, sigmoid_z * (1.0 + preact * (1.0 - sigmoid_z)))


def swap(value, row=0, col=0):
    rows, cols = lax.axis_size("row"), lax.axis_size("col")
    pairs = [(r * cols + c, (r ^ row) * cols + (c ^ col)) for r in range(rows) for c in range(cols)]
    return lax.ppermute(value, BOTH, pairs)


def limit(count):
    return 56 * 1024 * 1024 if count * 2 > 6 * 1024 * 1024 else 8 * 1024 * 1024


def front_kernel(cols_hbm, counts_hbm, tiles_hbm, feat_hbm, cot_hbm, bias_hbm, dense, dense_t, feat, cot, bias, cols, counts, tiles, sems):
    row_tiles, slots, tile, _ = tiles.shape
    me_row, me_col = lax.axis_index("row"), lax.axis_index("col")
    copies = [
        pltpu.make_async_copy(source, target, sems.at[i])
        for i, (source, target) in enumerate(
            (
                (cols_hbm.at[0, 0], cols),
                (counts_hbm.at[0], counts),
                (tiles_hbm.at[0, 0], tiles),
                (feat_hbm.at[0, 0], feat),
                (cot_hbm.at[0, 0], cot),
                (bias_hbm, bias),
            )
        )
    ]
    for copy in copies:
        copy.start()
    dense[...] = jnp.zeros(dense.shape, dense.dtype)
    dense_t[...] = jnp.zeros(dense_t.shape, dense_t.dtype)
    for copy in copies:
        copy.wait()

    def place(position):
        row_tile = position ^ me_col
        start = pl.multiple_of(position * tile, tile)
        for slot in range(slots):

            @pl.when(slot < counts[0, row_tile])
            def _():
                column = pl.multiple_of((cols[row_tile, slot] ^ me_row) * tile, tile)
                value = tiles[row_tile, slot]
                dense[pl.ds(start, tile), pl.ds(column, tile)] = value
                dense_t[pl.ds(column, tile), pl.ds(start, tile)] = value.T

    if row_tiles <= 8:
        for position in range(row_tiles):
            place(position)
    else:
        pl.loop(0, row_tiles)(place)


def front(tile_cols, tile_counts, tile_values, features, cotangent, out_bias):
    row_tiles, slots, tile, _ = tile_values.shape[2:]
    height, width = row_tiles * tile, lax.axis_size("row") * tile
    kind = tile_values.dtype
    return pl.pallas_call(
        front_kernel,
        in_specs=[HBM] * 6,
        out_shape=(
            jax.ShapeDtypeStruct((height, width), kind),
            jax.ShapeDtypeStruct((width, height), kind),
            jax.ShapeDtypeStruct(features.shape[2:], features.dtype),
            jax.ShapeDtypeStruct(cotangent.shape[2:], cotangent.dtype),
            jax.ShapeDtypeStruct((1, *out_bias.shape), out_bias.dtype),
        ),
        scratch_shapes=[
            pltpu.SMEM((row_tiles, slots), jnp.int32),
            pltpu.SMEM((1, row_tiles), jnp.int32),
            pltpu.VMEM((row_tiles, slots, tile, tile), kind),
            pltpu.SemaphoreType.DMA((6,)),
        ],
        compiler_params=pltpu.CompilerParams(vmem_limit_bytes=limit(height * width)),
        cost_estimate=pl.CostEstimate(flops=0, bytes_accessed=tile_values.size * 2, transcendentals=0),
    )(tile_cols, tile_counts, tile_values, features, cotangent, out_bias.reshape(1, -1))


def forward_kernel(count, *refs):
    pieces, (weight, dense), outs, projected = refs[:count], refs[count : count + 2], refs[count + 2 : -1], refs[-1]
    tile = pieces[0].shape[0]
    for j, piece in enumerate(pieces):
        value = jnp.dot(piece[...], weight[...], preferred_element_type=jnp.float32)
        projected[j * tile : (j + 1) * tile] = value.astype(projected.dtype)
    for p, out in enumerate(outs):
        value = jnp.dot(dense[p * tile : (p + 1) * tile], projected[...], preferred_element_type=jnp.float32)
        out[...] = value.astype(out.dtype)


def forward(pieces, weight, dense):
    tile, width = pieces[0].shape
    return pl.pallas_call(
        lambda *refs: forward_kernel(len(pieces), *refs),
        out_shape=[jax.ShapeDtypeStruct((tile, width), jnp.bfloat16)] * (dense.shape[0] // tile),
        scratch_shapes=[pltpu.VMEM((len(pieces) * tile, width), jnp.bfloat16)],
        compiler_params=pltpu.CompilerParams(vmem_limit_bytes=limit(dense.size)),
        cost_estimate=pl.CostEstimate(flops=2 * dense.size * width, bytes_accessed=0, transcendentals=0),
    )(*pieces, weight, dense)


def backward_kernel(count, *refs):
    pieces, dense_t, outs, grads = refs[:count], refs[count], refs[count + 1 : -1], refs[-1]
    tile = pieces[0].shape[0]
    for p, piece in enumerate(pieces):
        grads[p * tile : (p + 1) * tile] = piece[...]
    for j, out in enumerate(outs):
        value = jnp.dot(dense_t[j * tile : (j + 1) * tile], grads[...], preferred_element_type=jnp.float32)
        out[...] = value.astype(out.dtype)


def backward(pieces, dense_t):
    tile, width = pieces[0].shape
    return pl.pallas_call(
        lambda *refs: backward_kernel(len(pieces), *refs),
        out_shape=[jax.ShapeDtypeStruct((tile, width), jnp.bfloat16)] * (dense_t.shape[0] // tile),
        scratch_shapes=[pltpu.VMEM((len(pieces) * tile, width), jnp.bfloat16)],
        compiler_params=pltpu.CompilerParams(vmem_limit_bytes=limit(dense_t.size)),
        cost_estimate=pl.CostEstimate(flops=2 * dense_t.size * width, bytes_accessed=0, transcendentals=0),
    )(*pieces, dense_t)


def shards(features, weight, out_bias, tile_values, tile_cols, tile_counts, cotangent):
    far = lax.axis_size("col") // 2
    near = (3, 1, 2) if far == 4 else range(1, far)
    rows = range(1, lax.axis_size("row"))
    pieces = {s: swap(features[0, 0], row=s) for s in reversed(rows)}
    dense, dense_t, feat, cot, bias = front(
        tile_cols, tile_counts, tile_values, features, cotangent, out_bias
    )
    pieces[0] = feat
    product = forward([pieces[s] for s in range(len(pieces))], weight, dense)
    half = {}
    for p in (far, 0):
        total = product[p].astype(jnp.float32)
        for s in near:
            total = total + swap(product[p ^ s], col=s).astype(jnp.float32)
        half[p] = total
    other = swap(half[far].astype(jnp.bfloat16), col=far)
    preact = half[0] + other.astype(jnp.float32) + bias
    grads = {0: (cot.astype(jnp.float32) * silu_slope(preact)[1]).astype(jnp.bfloat16)}
    grads[far] = swap(grads[0], col=far)
    preact, grads[far] = lax.optimization_barrier((preact, grads[far]))
    activated = silu_slope(preact)[0].astype(jnp.bfloat16)
    for p in (0, far):
        for s in near:
            grads[p ^ s] = swap(grads[p], col=s)
    back = backward([grads[p] for p in range(2 * far)], dense_t)
    spread = back[0].astype(jnp.float32)
    for s in reversed(rows):
        spread = spread + swap(back[s], row=s).astype(jnp.float32)
    feature_grad = jnp.dot(spread.astype(jnp.bfloat16), weight.T, preferred_element_type=jnp.float32)
    return activated[None, None], feature_grad.astype(jnp.bfloat16)[None, None]


def solution(mesh):
    in_specs = (
        P("col", "row", None, None),
        P(),
        P(),
        P("row", "col", None, None, None, None),
        P("row", "col", None, None),
        P("row", "col", None),
        P("row", "col", None, None),
    )
    out_specs = (P("row", "col", None, None), P("col", "row", None, None))
    return jax.shard_map(shards, mesh=mesh, in_specs=in_specs, out_specs=out_specs, check_vma=False)
```

```python
import jax
import jax.numpy as jnp
from jax import lax
from jax.experimental import pallas as pl
from jax.experimental.pallas import tpu as pltpu
from jax.sharding import PartitionSpec as P

BOTH = ("row", "col")
HBM = pl.BlockSpec(memory_space=pltpu.HBM)


def silu_slope(preact):
    sigmoid_z = jax.nn.sigmoid(preact)
    return (preact * sigmoid_z, sigmoid_z * (1.0 + preact * (1.0 - sigmoid_z)))


def swap(value, row=0, col=0):
    rows, cols = lax.axis_size("row"), lax.axis_size("col")
    pairs = [(r * cols + c, (r ^ row) * cols + (c ^ col)) for r in range(rows) for c in range(cols)]
    return lax.ppermute(value, BOTH, pairs)


def limit(count):
    return 56 * 1024 * 1024 if count * 2 > 6 * 1024 * 1024 else 8 * 1024 * 1024


def dense_kernel(cols_hbm, counts_hbm, tiles_hbm, dense, cols, counts, tiles, sems):
    row_tiles, slots, tile, _ = tiles.shape
    me_row, me_col = lax.axis_index("row"), lax.axis_index("col")
    copies = [
        pltpu.make_async_copy(cols_hbm.at[0, 0], cols, sems.at[0]),
        pltpu.make_async_copy(counts_hbm.at[0], counts, sems.at[1]),
        pltpu.make_async_copy(tiles_hbm.at[0, 0], tiles, sems.at[2]),
    ]
    for copy in copies:
        copy.start()
    dense[...] = jnp.zeros(dense.shape, dense.dtype)
    for copy in copies:
        copy.wait()

    def place(position):
        row_tile = position ^ me_col
        start = pl.multiple_of(position * tile, tile)
        for slot in range(slots):

            @pl.when(slot < counts[0, row_tile])
            def _():
                column = pl.multiple_of((cols[row_tile, slot] ^ me_row) * tile, tile)
                dense[pl.ds(start, tile), pl.ds(column, tile)] = tiles[row_tile, slot]

    if row_tiles <= 8:
        for position in range(row_tiles):
            place(position)
    else:
        pl.loop(0, row_tiles)(place)


def dense_block(tile_cols, tile_counts, tile_values):
    row_tiles, slots, tile, _ = tile_values.shape[2:]
    height, width = row_tiles * tile, lax.axis_size("row") * tile
    kind = tile_values.dtype
    return pl.pallas_call(
        dense_kernel,
        in_specs=[HBM] * 3,
        out_shape=jax.ShapeDtypeStruct((height, width), kind),
        scratch_shapes=[
            pltpu.SMEM((row_tiles, slots), jnp.int32),
            pltpu.SMEM((1, row_tiles), jnp.int32),
            pltpu.VMEM((row_tiles, slots, tile, tile), kind),
            pltpu.SemaphoreType.DMA((3,)),
        ],
        compiler_params=pltpu.CompilerParams(vmem_limit_bytes=limit(height * width)),
        cost_estimate=pl.CostEstimate(flops=0, bytes_accessed=tile_values.size * 2, transcendentals=0),
    )(tile_cols, tile_counts, tile_values)


def forward_kernel(count, *refs):
    pieces, (weight, dense), outs, projected = refs[:count], refs[count : count + 2], refs[count + 2 : -1], refs[-1]
    tile = pieces[0].shape[0]
    for j, piece in enumerate(pieces):
        value = jnp.dot(piece[...], weight[...], preferred_element_type=jnp.float32)
        projected[j * tile : (j + 1) * tile] = value.astype(projected.dtype)
    for p, out in enumerate(outs):
        value = jnp.dot(dense[p * tile : (p + 1) * tile], projected[...], preferred_element_type=jnp.float32)
        out[...] = value.astype(out.dtype)


def forward(pieces, weight, dense):
    tile, width = pieces[0].shape
    return pl.pallas_call(
        lambda *refs: forward_kernel(len(pieces), *refs),
        out_shape=[jax.ShapeDtypeStruct((tile, width), jnp.bfloat16)] * (dense.shape[0] // tile),
        scratch_shapes=[pltpu.VMEM((len(pieces) * tile, width), jnp.bfloat16)],
        compiler_params=pltpu.CompilerParams(vmem_limit_bytes=limit(dense.size)),
        cost_estimate=pl.CostEstimate(flops=2 * dense.size * width, bytes_accessed=0, transcendentals=0),
    )(*pieces, weight, dense)


def backward_kernel(count, *refs):
    pieces, dense, outs, grads = refs[:count], refs[count], refs[count + 1 : -1], refs[-1]
    tile = pieces[0].shape[0]
    for p, piece in enumerate(pieces):
        grads[p * tile : (p + 1) * tile] = piece[...]
    for j, out in enumerate(outs):
        value = lax.dot_general(
            dense[:, j * tile : (j + 1) * tile], grads[...], (((0,), (0,)), ((), ())), preferred_element_type=jnp.float32
        )
        out[...] = value.astype(out.dtype)


def backward(pieces, dense):
    tile, width = pieces[0].shape
    return pl.pallas_call(
        lambda *refs: backward_kernel(len(pieces), *refs),
        out_shape=[jax.ShapeDtypeStruct((tile, width), jnp.bfloat16)] * (dense.shape[1] // tile),
        scratch_shapes=[pltpu.VMEM((len(pieces) * tile, width), jnp.bfloat16)],
        compiler_params=pltpu.CompilerParams(vmem_limit_bytes=limit(dense.size)),
        cost_estimate=pl.CostEstimate(flops=2 * dense.size * width, bytes_accessed=0, transcendentals=0),
    )(*pieces, dense)


def shards(features, weight, out_bias, tile_values, tile_cols, tile_counts, cotangent):
    far = lax.axis_size("col") // 2
    near = {k: v if far == 4 else range(1, far) for k, v in {'far': (3, 1, 2), 'own': (3, 1, 2), 'far grad': (2, 1, 3), 'own grad': (3, 1, 2)}.items()}
    rows = range(1, lax.axis_size("row"))
    own = features[0, 0]
    even = [s for s in rows if s % 2 == 0]
    pieces = {s: swap(own, row=s) for s in even}
    pieces[0] = own
    pieces[1] = swap(own, row=1)
    dense = dense_block(tile_cols, tile_counts, tile_values)
    dense, *got = lax.optimization_barrier((dense, *(pieces[s] for s in even)))
    for s, piece in zip(even, got):
        pieces[s] = piece
        pieces[s + 1] = swap(piece, row=1)
    product = forward([pieces[s] for s in range(len(pieces))], weight, dense)
    half = {}
    for p in (far, 0):
        total = product[p].astype(jnp.float32)
        for s in near["far" if p else "own"]:
            total = total + swap(product[p ^ s], col=s).astype(jnp.float32)
        half[p] = total
    other = swap(half[far].astype(jnp.bfloat16), col=far)
    preact = half[0] + other.astype(jnp.float32) + out_bias
    grads = {0: (cotangent[0, 0].astype(jnp.float32) * silu_slope(preact)[1]).astype(jnp.bfloat16)}
    grads[far] = swap(grads[0], col=far)
    preact, grads[far] = lax.optimization_barrier((preact, grads[far]))
    activated = silu_slope(preact)[0].astype(jnp.bfloat16)
    for p in (0, far):
        for s in near["far grad" if p else "own grad"]:
            grads[p ^ s] = swap(grads[p], col=s)
    back = backward([grads[p] for p in range(2 * far)], dense)
    spread = back[0].astype(jnp.float32)
    for s in (2, 1, 3):
        spread = spread + swap(back[s], row=s).astype(jnp.float32)
    feature_grad = jnp.dot(spread.astype(jnp.bfloat16), weight.T, preferred_element_type=jnp.float32)
    return activated[None, None], feature_grad.astype(jnp.bfloat16)[None, None]


def solution(mesh):
    in_specs = (
        P("col", "row", None, None),
        P(),
        P(),
        P("row", "col", None, None, None, None),
        P("row", "col", None, None),
        P("row", "col", None),
        P("row", "col", None, None),
    )
    out_specs = (P("row", "col", None, None), P("col", "row", None, None))
    return jax.shard_map(shards, mesh=mesh, in_specs=in_specs, out_specs=out_specs, check_vma=False)
```

```python
import jax
import jax.numpy as jnp
from jax import lax
from jax.experimental import pallas as pl
from jax.experimental.pallas import tpu as pltpu
from jax.sharding import PartitionSpec as P

BOTH = ("row", "col")
HBM = pl.BlockSpec(memory_space=pltpu.HBM)


def silu_slope(preact):
    sigmoid_z = jax.nn.sigmoid(preact)
    return (preact * sigmoid_z, sigmoid_z * (1.0 + preact * (1.0 - sigmoid_z)))


def swap(value, row=0, col=0):
    rows, cols = lax.axis_size("row"), lax.axis_size("col")
    pairs = [(r * cols + c, (r ^ row) * cols + (c ^ col)) for r in range(rows) for c in range(cols)]
    return lax.ppermute(value, BOTH, pairs)


def limit(count):
    return 56 * 1024 * 1024 if count * 2 > 6 * 1024 * 1024 else 8 * 1024 * 1024


def dense_kernel(cols_hbm, counts_hbm, tiles_hbm, dense, cols, counts, tiles, sems):
    row_tiles, slots, tile, _ = tiles.shape
    me_row, me_col = lax.axis_index("row"), lax.axis_index("col")
    copies = [
        pltpu.make_async_copy(cols_hbm.at[0, 0], cols, sems.at[0]),
        pltpu.make_async_copy(counts_hbm.at[0], counts, sems.at[1]),
        pltpu.make_async_copy(tiles_hbm.at[0, 0], tiles, sems.at[2]),
    ]
    for copy in copies:
        copy.start()
    dense[...] = jnp.zeros(dense.shape, dense.dtype)
    for copy in copies:
        copy.wait()

    def place(position):
        row_tile = position ^ me_col
        start = pl.multiple_of(position * tile, tile)
        for slot in range(slots):

            @pl.when(slot < counts[0, row_tile])
            def _():
                column = pl.multiple_of((cols[row_tile, slot] ^ me_row) * tile, tile)
                dense[pl.ds(start, tile), pl.ds(column, tile)] = tiles[row_tile, slot]

    if row_tiles <= 8:
        for position in range(row_tiles):
            place(position)
    else:
        pl.loop(0, row_tiles)(place)


def dense_block(tile_cols, tile_counts, tile_values):
    row_tiles, slots, tile, _ = tile_values.shape[2:]
    height, width = row_tiles * tile, lax.axis_size("row") * tile
    kind = tile_values.dtype
    return pl.pallas_call(
        dense_kernel,
        in_specs=[HBM] * 3,
        out_shape=jax.ShapeDtypeStruct((height, width), kind),
        scratch_shapes=[
            pltpu.SMEM((row_tiles, slots), jnp.int32),
            pltpu.SMEM((1, row_tiles), jnp.int32),
            pltpu.VMEM((row_tiles, slots, tile, tile), kind),
            pltpu.SemaphoreType.DMA((3,)),
        ],
        compiler_params=pltpu.CompilerParams(vmem_limit_bytes=limit(height * width)),
        cost_estimate=pl.CostEstimate(flops=0, bytes_accessed=tile_values.size * 2, transcendentals=0),
    )(tile_cols, tile_counts, tile_values)


def project_kernel(places, count, *refs):
    pieces, (weight, dense), (projected, *outs) = refs[:count], refs[count : count + 2], refs[count + 2 :]
    tile = pieces[0].shape[0]
    for j, piece in enumerate(pieces):
        value = jnp.dot(piece[...], weight[...], preferred_element_type=jnp.float32)
        projected[j * tile : (j + 1) * tile] = value.astype(projected.dtype)
    product_kernel(places, projected, dense, *outs)


def product_kernel(places, projected, dense, *outs):
    tile = outs[0].shape[0]
    for p, out in zip(places, outs):
        value = jnp.dot(dense[p * tile : (p + 1) * tile], projected[...], preferred_element_type=jnp.float32)
        out[...] = value.astype(out.dtype)


def forward(pieces, weight, dense, far):
    tile, width = pieces[0].shape
    params = pltpu.CompilerParams(vmem_limit_bytes=limit(dense.size))
    cost = pl.CostEstimate(flops=dense.size * width, bytes_accessed=0, transcendentals=0)
    out = [jax.ShapeDtypeStruct((tile, width), jnp.bfloat16)] * far
    last, first = range(far), range(far, 2 * far)
    projected, *outs = pl.pallas_call(
        lambda *refs: project_kernel(first, len(pieces), *refs),
        out_shape=[jax.ShapeDtypeStruct((len(pieces) * tile, width), jnp.bfloat16), *out],
        compiler_params=params,
        cost_estimate=cost,
    )(*pieces, weight, dense)
    product = dict(zip(first, outs))
    outs = pl.pallas_call(
        lambda *refs: product_kernel(last, *refs), out_shape=out, compiler_params=params, cost_estimate=cost
    )(projected, dense)
    return {**product, **dict(zip(last, outs))}


def backward_kernel(places, *refs):
    count = len(places)
    pieces, dense, outs, grads = refs[:count], refs[count], refs[count + 1 : -1], refs[-1]
    tile = pieces[0].shape[1]
    half = grads.shape[0] // 2
    for p, piece in zip(places, pieces):
        grads[p * tile : (p + 1) * tile] = piece[0]
        grads[half + p * tile : half + (p + 1) * tile] = piece[1]
    for j, out in enumerate(outs):
        value = lax.dot_general(
            dense[:, j * tile : (j + 1) * tile], grads[...], (((0,), (0,)), ((), ())), preferred_element_type=jnp.float32
        )
        out[...] = value.astype(out.dtype)


def backward(places, pieces, dense):
    _, tile, width = pieces[0].shape
    return pl.pallas_call(
        lambda *refs: backward_kernel(places, *refs),
        out_shape=[jax.ShapeDtypeStruct((tile, width), jnp.bfloat16)] * (dense.shape[1] // tile),
        scratch_shapes=[pltpu.VMEM((2 * len(pieces) * tile, width), jnp.bfloat16)],
        compiler_params=pltpu.CompilerParams(vmem_limit_bytes=limit(dense.size)),
        cost_estimate=pl.CostEstimate(flops=2 * dense.size * width, bytes_accessed=0, transcendentals=0),
    )(*pieces, dense)


def shards(features, weight, out_bias, tile_values, tile_cols, tile_counts, cotangent):
    far = lax.axis_size("col") // 2
    near = {k: v if far == 4 else range(1, far) for k, v in {'far': (3, 2, 1), 'own': (3, 1, 2)}.items()}
    rows = range(1, lax.axis_size("row"))
    own = features[0, 0]
    even = [s for s in rows if s % 2 == 0]
    pieces = {s: swap(own, row=s) for s in even}
    pieces[0] = own
    pieces[1] = swap(own, row=1)
    dense = dense_block(tile_cols, tile_counts, tile_values)
    dense, *got = lax.optimization_barrier((dense, *(pieces[s] for s in even)))
    for s, piece in zip(even, got):
        pieces[s] = piece
        pieces[s + 1] = swap(piece, row=1)
    product = forward([pieces[s] for s in range(len(pieces))], weight, dense, far)
    half = {}
    for p in (far, 0):
        total = product[p].astype(jnp.float32)
        for s in near["far" if p else "own"]:
            total = total + swap(product[p ^ s], col=s).astype(jnp.float32)
        half[p] = total
    other = swap(half[far].astype(jnp.bfloat16), col=far)
    preact = half[0] + other.astype(jnp.float32) + out_bias
    grads = {0: (cotangent[0, 0].astype(jnp.float32) * silu_slope(preact)[1]).astype(jnp.bfloat16)}
    grads[far] = swap(grads[0], col=far)
    preact, grads[far] = lax.optimization_barrier((preact, grads[far]))
    activated = silu_slope(preact)[0].astype(jnp.bfloat16)
    pair = jnp.stack([grads[0], grads[far]])
    places = [1, 2, 3, 0] if far == 4 else list(range(far))
    back = backward(places, [swap(pair, col=p) if p else pair for p in places], dense)
    spread = back[0].astype(jnp.float32)
    for s in ((2, 1, 3) if len(rows) == 3 else rows):
        spread = spread + swap(back[s], row=s).astype(jnp.float32)
    feature_grad = jnp.dot(spread.astype(jnp.bfloat16), weight.T, preferred_element_type=jnp.float32)
    return activated[None, None], feature_grad.astype(jnp.bfloat16)[None, None]


def solution(mesh):
    in_specs = (
        P("col", "row", None, None),
        P(),
        P(),
        P("row", "col", None, None, None, None),
        P("row", "col", None, None),
        P("row", "col", None),
        P("row", "col", None, None),
    )
    out_specs = (P("row", "col", None, None), P("col", "row", None, None))
    return jax.shard_map(shards, mesh=mesh, in_specs=in_specs, out_specs=out_specs, check_vma=False)
```

```python
import jax
import jax.numpy as jnp
from jax import lax
from jax.experimental import pallas as pl
from jax.experimental.pallas import tpu as pltpu
from jax.sharding import PartitionSpec as P

BOTH = ("row", "col")
HBM = pl.BlockSpec(memory_space=pltpu.HBM)


def silu_slope(preact):
    sigmoid_z = jax.nn.sigmoid(preact)
    return (preact * sigmoid_z, sigmoid_z * (1.0 + preact * (1.0 - sigmoid_z)))


def swap(value, row=0, col=0):
    rows, cols = lax.axis_size("row"), lax.axis_size("col")
    pairs = [(r * cols + c, (r ^ row) * cols + (c ^ col)) for r in range(rows) for c in range(cols)]
    return lax.ppermute(value, BOTH, pairs)


def limit(count):
    return 56 * 1024 * 1024 if count * 2 > 6 * 1024 * 1024 else 8 * 1024 * 1024


def dense_kernel(cols_hbm, counts_hbm, tiles_hbm, dense, cols, counts, tiles, sems):
    row_tiles, slots, tile, _ = tiles.shape
    width = dense.shape[1]
    me_row, me_col = lax.axis_index("row"), lax.axis_index("col")
    copies = [
        pltpu.make_async_copy(cols_hbm.at[0, 0], cols, sems.at[0]),
        pltpu.make_async_copy(counts_hbm.at[0], counts, sems.at[1]),
        pltpu.make_async_copy(tiles_hbm.at[0, 0], tiles, sems.at[2]),
    ]
    for copy in copies:
        copy.start()
    dense[...] = jnp.zeros(dense.shape, dense.dtype)
    for copy in copies:
        copy.wait()

    def place(position):
        row_tile = position ^ me_col
        start = pl.multiple_of(position * tile, tile)
        for slot in range(slots):

            @pl.when(slot < counts[0, row_tile])
            def _():
                peer = cols[row_tile, slot] ^ me_row
                column = pl.multiple_of((peer // 2 + peer % 2 * (width // tile // 2)) * tile, tile)
                dense[pl.ds(start, tile), pl.ds(column, tile)] = tiles[row_tile, slot]

    if row_tiles <= 8:
        for position in range(row_tiles):
            place(position)
    else:
        pl.loop(0, row_tiles)(place)


def dense_block(tile_cols, tile_counts, tile_values):
    row_tiles, slots, tile, _ = tile_values.shape[2:]
    height, width = row_tiles * tile, lax.axis_size("row") * tile
    kind = tile_values.dtype
    return pl.pallas_call(
        dense_kernel,
        in_specs=[HBM] * 3,
        out_shape=jax.ShapeDtypeStruct((height, width), kind),
        scratch_shapes=[
            pltpu.SMEM((row_tiles, slots), jnp.int32),
            pltpu.SMEM((1, row_tiles), jnp.int32),
            pltpu.VMEM((row_tiles, slots, tile, tile), kind),
            pltpu.SemaphoreType.DMA((3,)),
        ],
        compiler_params=pltpu.CompilerParams(vmem_limit_bytes=limit(height * width)),
        cost_estimate=pl.CostEstimate(flops=0, bytes_accessed=tile_values.size * 2, transcendentals=0),
    )(tile_cols, tile_counts, tile_values)


def start_kernel(count, *refs):
    pieces, (weight, dense), (projected, begun) = refs[:count], refs[count : count + 2], refs[count + 2 :]
    tile, far = pieces[0].shape[0], begun.shape[0]
    for j, piece in enumerate(pieces):
        value = jnp.dot(piece[...], weight[...], preferred_element_type=jnp.float32)
        projected[j * tile : (j + 1) * tile] = value.astype(projected.dtype)
    for k in range(far):
        begun[k] = jnp.dot(
            dense[(far + k) * tile : (far + k + 1) * tile, : count * tile],
            projected[...],
            preferred_element_type=jnp.float32,
        )


def finish_kernel(count, *refs):
    pieces, (weight, dense, begun), (projected, *outs) = refs[:count], refs[count : count + 3], refs[count + 3 :]
    tile, far = pieces[0].shape[0], begun.shape[0]
    for j, piece in enumerate(pieces):
        value = jnp.dot(piece[...], weight[...], preferred_element_type=jnp.float32)
        projected[j * tile : (j + 1) * tile] = value.astype(projected.dtype)
    for k, out in enumerate(outs):
        value = jnp.dot(
            dense[(far + k) * tile : (far + k + 1) * tile, count * tile :],
            projected[...],
            preferred_element_type=jnp.float32,
        )
        out[...] = (begun[k] + value).astype(out.dtype)


def product_kernel(first, second, dense, *outs):
    tile, width = outs[0].shape[0], first.shape[0]
    for p, out in enumerate(outs):
        rows = dense[p * tile : (p + 1) * tile]
        value = jnp.dot(rows[:, :width], first[...], preferred_element_type=jnp.float32)
        value = value + jnp.dot(rows[:, width:], second[...], preferred_element_type=jnp.float32)
        out[...] = value.astype(out.dtype)


def start(pieces, weight, dense, far):
    tile, width = pieces[0].shape
    return pl.pallas_call(
        lambda *refs: start_kernel(len(pieces), *refs),
        out_shape=(
            jax.ShapeDtypeStruct((len(pieces) * tile, width), jnp.bfloat16),
            jax.ShapeDtypeStruct((far, tile, width), jnp.float32),
        ),
        compiler_params=pltpu.CompilerParams(vmem_limit_bytes=limit(dense.size)),
        cost_estimate=pl.CostEstimate(flops=dense.size * width // 2, bytes_accessed=0, transcendentals=0),
    )(*pieces, weight, dense)


def forward(begun, pieces, weight, dense, far):
    first, begun = begun
    tile, width = pieces[0].shape
    params = pltpu.CompilerParams(vmem_limit_bytes=limit(dense.size))
    out = [jax.ShapeDtypeStruct((tile, width), jnp.bfloat16)] * far
    second, *outs = pl.pallas_call(
        lambda *refs: finish_kernel(len(pieces), *refs),
        out_shape=[jax.ShapeDtypeStruct((len(pieces) * tile, width), jnp.bfloat16), *out],
        compiler_params=params,
        cost_estimate=pl.CostEstimate(flops=dense.size * width // 2, bytes_accessed=0, transcendentals=0),
    )(*pieces, weight, dense, begun)
    product = {far + k: value for k, value in enumerate(outs)}
    outs = pl.pallas_call(
        product_kernel,
        out_shape=out,
        compiler_params=params,
        cost_estimate=pl.CostEstimate(flops=dense.size * width, bytes_accessed=0, transcendentals=0),
    )(first, second, dense)
    return {**product, **dict(enumerate(outs))}


def backward_kernel(places, *refs):
    count = len(places)
    pieces, dense, outs, grads = refs[:count], refs[count], refs[count + 1 : -1], refs[-1]
    tile = pieces[0].shape[1]
    half = grads.shape[0] // 2
    for p, piece in zip(places, pieces):
        grads[p * tile : (p + 1) * tile] = piece[0]
        grads[half + p * tile : half + (p + 1) * tile] = piece[1]
    for j, out in enumerate(outs):
        value = lax.dot_general(
            dense[:, j * tile : (j + 1) * tile], grads[...], (((0,), (0,)), ((), ())), preferred_element_type=jnp.float32
        )
        out[...] = value.astype(out.dtype)


def backward(places, pieces, dense):
    _, tile, width = pieces[0].shape
    return pl.pallas_call(
        lambda *refs: backward_kernel(places, *refs),
        out_shape=[jax.ShapeDtypeStruct((tile, width), jnp.bfloat16)] * (dense.shape[1] // tile),
        scratch_shapes=[pltpu.VMEM((2 * len(pieces) * tile, width), jnp.bfloat16)],
        compiler_params=pltpu.CompilerParams(vmem_limit_bytes=limit(dense.size)),
        cost_estimate=pl.CostEstimate(flops=2 * dense.size * width, bytes_accessed=0, transcendentals=0),
    )(*pieces, dense)


def shards(features, weight, out_bias, tile_values, tile_cols, tile_counts, cotangent):
    far = lax.axis_size("col") // 2
    near = {"far": (3, 2, 1), "own": (3, 1, 2)} if far == 4 else {"far": range(1, far), "own": range(1, far)}
    rows = range(1, lax.axis_size("row"))
    own = features[0, 0]
    even = [s for s in rows if s % 2 == 0]
    pieces = {s: swap(own, row=s) for s in even}
    pieces[0] = own
    pieces[1] = swap(own, row=1)
    dense = dense_block(tile_cols, tile_counts, tile_values)
    dense, *got = lax.optimization_barrier((dense, *(pieces[s] for s in even)))
    twins = [swap(piece, row=1) for piece in got]
    begun = start([own, *got], weight, dense, far)
    product = forward(begun, [pieces[1], *twins], weight, dense, far)
    half = {}
    for p in (far, 0):
        total = product[p].astype(jnp.float32)
        for s in near["far" if p else "own"]:
            total = total + swap(product[p ^ s], col=s).astype(jnp.float32)
        half[p] = total
    other = swap(half[far].astype(jnp.bfloat16), col=far)
    preact = half[0] + other.astype(jnp.float32) + out_bias
    grads = {0: (cotangent[0, 0].astype(jnp.float32) * silu_slope(preact)[1]).astype(jnp.bfloat16)}
    grads[far] = swap(grads[0], col=far)
    preact, grads[far] = lax.optimization_barrier((preact, grads[far]))
    activated = silu_slope(preact)[0].astype(jnp.bfloat16)
    pair = jnp.stack([grads[0], grads[far]])
    places = [1, 2, 3, 0] if far == 4 else list(range(far))
    back = backward(places, [swap(pair, col=p) if p else pair for p in places], dense)
    back = dict(zip([0, *even, *(s for s in rows if s % 2)], back))
    spread = back[0].astype(jnp.float32)
    for s in ((2, 1, 3) if len(rows) == 3 else rows):
        spread = spread + swap(back[s], row=s).astype(jnp.float32)
    feature_grad = jnp.dot(spread.astype(jnp.bfloat16), weight.T, preferred_element_type=jnp.float32)
    return activated[None, None], feature_grad.astype(jnp.bfloat16)[None, None]


def solution(mesh):
    in_specs = (
        P("col", "row", None, None),
        P(),
        P(),
        P("row", "col", None, None, None, None),
        P("row", "col", None, None),
        P("row", "col", None),
        P("row", "col", None, None),
    )
    out_specs = (P("row", "col", None, None), P("col", "row", None, None))
    return jax.shard_map(shards, mesh=mesh, in_specs=in_specs, out_specs=out_specs, check_vma=False)
```

```python
import jax
import jax.numpy as jnp
from jax import lax
from jax.experimental import pallas as pl
from jax.experimental.pallas import tpu as pltpu
from jax.sharding import PartitionSpec as P

BOTH = ("row", "col")
HBM = pl.BlockSpec(memory_space=pltpu.HBM)


def silu_slope(preact):
    sigmoid_z = jax.nn.sigmoid(preact)
    return (preact * sigmoid_z, sigmoid_z * (1.0 + preact * (1.0 - sigmoid_z)))


def swap(value, row=0, col=0):
    rows, cols = lax.axis_size("row"), lax.axis_size("col")
    pairs = [(r * cols + c, (r ^ row) * cols + (c ^ col)) for r in range(rows) for c in range(cols)]
    return lax.ppermute(value, BOTH, pairs)


def limit(count):
    return 56 * 1024 * 1024 if count * 2 > 6 * 1024 * 1024 else 8 * 1024 * 1024


def dense_kernel(cols_hbm, counts_hbm, tiles_hbm, dense, cols, counts, tiles, sems):
    row_tiles, slots, tile, _ = tiles.shape
    width = dense.shape[1]
    me_row, me_col = lax.axis_index("row"), lax.axis_index("col")
    copies = [
        pltpu.make_async_copy(cols_hbm.at[0, 0], cols, sems.at[0]),
        pltpu.make_async_copy(counts_hbm.at[0], counts, sems.at[1]),
        pltpu.make_async_copy(tiles_hbm.at[0, 0], tiles, sems.at[2]),
    ]
    for copy in copies:
        copy.start()
    dense[...] = jnp.zeros(dense.shape, dense.dtype)
    for copy in copies:
        copy.wait()

    def place(position):
        row_tile = position ^ me_col
        start = pl.multiple_of(position * tile, tile)
        for slot in range(slots):

            @pl.when(slot < counts[0, row_tile])
            def _():
                peer = cols[row_tile, slot] ^ me_row
                column = pl.multiple_of((peer // 2 + peer % 2 * (width // tile // 2)) * tile, tile)
                dense[pl.ds(start, tile), pl.ds(column, tile)] = tiles[row_tile, slot]

    if row_tiles <= 8:
        for position in range(row_tiles):
            place(position)
    else:
        pl.loop(0, row_tiles)(place)


def dense_block(tile_cols, tile_counts, tile_values):
    row_tiles, slots, tile, _ = tile_values.shape[2:]
    height, width = row_tiles * tile, lax.axis_size("row") * tile
    kind = tile_values.dtype
    return pl.pallas_call(
        dense_kernel,
        in_specs=[HBM] * 3,
        out_shape=jax.ShapeDtypeStruct((height, width), kind),
        scratch_shapes=[
            pltpu.SMEM((row_tiles, slots), jnp.int32),
            pltpu.SMEM((1, row_tiles), jnp.int32),
            pltpu.VMEM((row_tiles, slots, tile, tile), kind),
            pltpu.SemaphoreType.DMA((3,)),
        ],
        compiler_params=pltpu.CompilerParams(vmem_limit_bytes=limit(height * width)),
        cost_estimate=pl.CostEstimate(flops=0, bytes_accessed=tile_values.size * 2, transcendentals=0),
    )(tile_cols, tile_counts, tile_values)


def start_kernel(count, *refs):
    pieces, (weight, dense), (projected, begun) = refs[:count], refs[count : count + 2], refs[count + 2 :]
    tile, far = pieces[0].shape[0], begun.shape[0]
    for j, piece in enumerate(pieces):
        value = jnp.dot(piece[...], weight[...], preferred_element_type=jnp.float32)
        projected[j * tile : (j + 1) * tile] = value.astype(projected.dtype)
    for k in range(far):
        begun[k] = jnp.dot(
            dense[(far + k) * tile : (far + k + 1) * tile, : count * tile],
            projected[...],
            preferred_element_type=jnp.float32,
        )


def finish_kernel(count, *refs):
    pieces, (weight, dense, begun), (projected, *outs) = refs[:count], refs[count : count + 3], refs[count + 3 :]
    tile, far = pieces[0].shape[0], begun.shape[0]
    for j, piece in enumerate(pieces):
        value = jnp.dot(piece[...], weight[...], preferred_element_type=jnp.float32)
        projected[j * tile : (j + 1) * tile] = value.astype(projected.dtype)
    for k, out in enumerate(outs):
        value = jnp.dot(
            dense[(far + k) * tile : (far + k + 1) * tile, count * tile :],
            projected[...],
            preferred_element_type=jnp.float32,
        )
        out[...] = (begun[k] + value).astype(out.dtype)


def product_kernel(first, second, dense, *outs):
    tile, width = outs[0].shape[0], first.shape[0]
    for p, out in enumerate(outs):
        rows = dense[p * tile : (p + 1) * tile]
        value = jnp.dot(rows[:, :width], first[...], preferred_element_type=jnp.float32)
        value = value + jnp.dot(rows[:, width:], second[...], preferred_element_type=jnp.float32)
        out[...] = value.astype(out.dtype)


def start(pieces, weight, dense, far):
    tile, width = pieces[0].shape
    return pl.pallas_call(
        lambda *refs: start_kernel(len(pieces), *refs),
        out_shape=(
            jax.ShapeDtypeStruct((len(pieces) * tile, width), jnp.bfloat16),
            jax.ShapeDtypeStruct((far, tile, width), jnp.float32),
        ),
        compiler_params=pltpu.CompilerParams(vmem_limit_bytes=limit(dense.size)),
        cost_estimate=pl.CostEstimate(flops=dense.size * width // 2, bytes_accessed=0, transcendentals=0),
    )(*pieces, weight, dense)


def forward(begun, pieces, weight, dense, far):
    first, begun = begun
    tile, width = pieces[0].shape
    params = pltpu.CompilerParams(vmem_limit_bytes=limit(dense.size))
    out = [jax.ShapeDtypeStruct((tile, width), jnp.bfloat16)] * far
    second, *outs = pl.pallas_call(
        lambda *refs: finish_kernel(len(pieces), *refs),
        out_shape=[jax.ShapeDtypeStruct((len(pieces) * tile, width), jnp.bfloat16), *out],
        compiler_params=params,
        cost_estimate=pl.CostEstimate(flops=dense.size * width // 2, bytes_accessed=0, transcendentals=0),
    )(*pieces, weight, dense, begun)
    product = {far + k: value for k, value in enumerate(outs)}
    outs = pl.pallas_call(
        product_kernel,
        out_shape=out,
        compiler_params=params,
        cost_estimate=pl.CostEstimate(flops=dense.size * width, bytes_accessed=0, transcendentals=0),
    )(first, second, dense)
    return {**product, **dict(enumerate(outs))}


def backward_kernel(places, *refs):
    count = len(places)
    pieces, (dense, weight), outs, grads = refs[:count], refs[count : count + 2], refs[count + 2 : -1], refs[-1]
    tile = pieces[0].shape[1]
    half = grads.shape[0] // 2
    for p, piece in zip(places, pieces):
        grads[p * tile : (p + 1) * tile] = piece[0]
        grads[half + p * tile : half + (p + 1) * tile] = piece[1]
    for j, out in enumerate(outs):
        value = lax.dot_general(
            dense[:, j * tile : (j + 1) * tile], grads[...], (((0,), (0,)), ((), ())), preferred_element_type=jnp.float32
        )
        if j > len(outs) // 2:
            value = lax.dot_general(
                value.astype(out.dtype), weight[...], (((1,), (1,)), ((), ())), preferred_element_type=jnp.float32
            )
        out[...] = value.astype(out.dtype)


def backward(places, pieces, dense, weight):
    _, tile, width = pieces[0].shape
    return pl.pallas_call(
        lambda *refs: backward_kernel(places, *refs),
        out_shape=[jax.ShapeDtypeStruct((tile, width), jnp.bfloat16)] * (dense.shape[1] // tile),
        scratch_shapes=[pltpu.VMEM((2 * len(pieces) * tile, width), jnp.bfloat16)],
        compiler_params=pltpu.CompilerParams(vmem_limit_bytes=limit(dense.size)),
        cost_estimate=pl.CostEstimate(flops=2 * dense.size * width, bytes_accessed=0, transcendentals=0),
    )(*pieces, dense, weight)


def shards(features, weight, out_bias, tile_values, tile_cols, tile_counts, cotangent):
    far = lax.axis_size("col") // 2
    near = {"far": (3, 2, 1), "own": (3, 1, 2)} if far == 4 else {"far": range(1, far), "own": range(1, far)}
    rows = range(1, lax.axis_size("row"))
    own = features[0, 0]
    even = [s for s in rows if s % 2 == 0]
    pieces = {s: swap(own, row=s) for s in even}
    pieces[0] = own
    pieces[1] = swap(own, row=1)
    dense = dense_block(tile_cols, tile_counts, tile_values)
    dense, *got = lax.optimization_barrier((dense, *(pieces[s] for s in even)))
    twins = [swap(piece, row=1) for piece in got]
    begun = start([own, *got], weight, dense, far)
    product = forward(begun, [pieces[1], *twins], weight, dense, far)
    half = {}
    for p in (far, 0):
        total = product[p].astype(jnp.float32)
        for s in near["far" if p else "own"]:
            total = total + swap(product[p ^ s], col=s).astype(jnp.float32)
        half[p] = total
    other = swap(half[far].astype(jnp.bfloat16), col=far)
    preact = half[0] + other.astype(jnp.float32) + out_bias
    grads = {0: (cotangent[0, 0].astype(jnp.float32) * silu_slope(preact)[1]).astype(jnp.bfloat16)}
    grads[far] = swap(grads[0], col=far)
    preact, grads[far] = lax.optimization_barrier((preact, grads[far]))
    activated = silu_slope(preact)[0].astype(jnp.bfloat16)
    pair = jnp.stack([grads[0], grads[far]])
    places = [1, 2, 3, 0] if far == 4 else list(range(far))
    messages = [swap(pair, col=p) if p else pair for p in places]
    messages[0], activated = lax.optimization_barrier((messages[0], activated))
    back = backward(places, messages, dense, weight)
    back = dict(zip([0, *even, *(s for s in rows if s % 2)], back))
    spread = back[0].astype(jnp.float32)
    for s in (*even, 1):
        spread = spread + swap(back[s], row=s).astype(jnp.float32)
    ready = jnp.dot(spread.astype(jnp.bfloat16), weight.T, preferred_element_type=jnp.float32)
    ready = lax.optimization_barrier(ready)
    for s in even:
        ready = ready + swap(back[s + 1], row=s + 1).astype(jnp.float32)
    return activated[None, None], ready.astype(jnp.bfloat16)[None, None]


def solution(mesh):
    in_specs = (
        P("col", "row", None, None),
        P(),
        P(),
        P("row", "col", None, None, None, None),
        P("row", "col", None, None),
        P("row", "col", None),
        P("row", "col", None, None),
    )
    out_specs = (P("row", "col", None, None), P("col", "row", None, None))
    return jax.shard_map(shards, mesh=mesh, in_specs=in_specs, out_specs=out_specs, check_vma=False)
```

```python
import jax
import jax.numpy as jnp
from jax import lax
from jax.experimental import pallas as pl
from jax.experimental.pallas import tpu as pltpu
from jax.sharding import PartitionSpec as P

BOTH = ("row", "col")
HBM = pl.BlockSpec(memory_space=pltpu.HBM)


def silu_slope(preact):
    sigmoid_z = jax.nn.sigmoid(preact)
    return (preact * sigmoid_z, sigmoid_z * (1.0 + preact * (1.0 - sigmoid_z)))


def swap(value, row=0, col=0):
    rows, cols = lax.axis_size("row"), lax.axis_size("col")
    pairs = [(r * cols + c, (r ^ row) * cols + (c ^ col)) for r in range(rows) for c in range(cols)]
    return lax.ppermute(value, BOTH, pairs)


def limit(count):
    return 56 * 1024 * 1024 if count * 2 > 6 * 1024 * 1024 else 8 * 1024 * 1024


def dense_kernel(cols_hbm, counts_hbm, tiles_hbm, dense, cols, counts, tiles, sems):
    row_tiles, slots, tile, _ = tiles.shape
    width = dense.shape[1]
    me_row, me_col = lax.axis_index("row"), lax.axis_index("col")
    copies = [
        pltpu.make_async_copy(cols_hbm.at[0, 0], cols, sems.at[0]),
        pltpu.make_async_copy(counts_hbm.at[0], counts, sems.at[1]),
        pltpu.make_async_copy(tiles_hbm.at[0, 0], tiles, sems.at[2]),
    ]
    for copy in copies:
        copy.start()
    dense[...] = jnp.zeros(dense.shape, dense.dtype)
    for copy in copies:
        copy.wait()

    def place(position):
        row_tile = position ^ me_col
        start = pl.multiple_of(position * tile, tile)
        for slot in range(slots):

            @pl.when(slot < counts[0, row_tile])
            def _():
                peer = cols[row_tile, slot] ^ me_row
                column = pl.multiple_of((peer // 2 + peer % 2 * (width // tile // 2)) * tile, tile)
                dense[pl.ds(start, tile), pl.ds(column, tile)] = tiles[row_tile, slot]

    if row_tiles <= 8:
        for position in range(row_tiles):
            place(position)
    else:
        pl.loop(0, row_tiles)(place)


def dense_block(tile_cols, tile_counts, tile_values):
    row_tiles, slots, tile, _ = tile_values.shape[2:]
    height, width = row_tiles * tile, lax.axis_size("row") * tile
    kind = tile_values.dtype
    return pl.pallas_call(
        dense_kernel,
        in_specs=[HBM] * 3,
        out_shape=jax.ShapeDtypeStruct((height, width), kind),
        scratch_shapes=[
            pltpu.SMEM((row_tiles, slots), jnp.int32),
            pltpu.SMEM((1, row_tiles), jnp.int32),
            pltpu.VMEM((row_tiles, slots, tile, tile), kind),
            pltpu.SemaphoreType.DMA((3,)),
        ],
        compiler_params=pltpu.CompilerParams(vmem_limit_bytes=limit(height * width)),
        cost_estimate=pl.CostEstimate(flops=0, bytes_accessed=tile_values.size * 2, transcendentals=0),
    )(tile_cols, tile_counts, tile_values)


def start_kernel(count, *refs):
    pieces, (weight, dense), (projected, begun) = refs[:count], refs[count : count + 2], refs[count + 2 :]
    tile, far = pieces[0].shape[0], begun.shape[0]
    for j, piece in enumerate(pieces):
        value = jnp.dot(piece[...], weight[...], preferred_element_type=jnp.float32)
        projected[j * tile : (j + 1) * tile] = value.astype(projected.dtype)
    for k in range(far):
        begun[k] = jnp.dot(
            dense[(far + k) * tile : (far + k + 1) * tile, : count * tile],
            projected[...],
            preferred_element_type=jnp.float32,
        )


def finish_kernel(count, *refs):
    pieces, (weight, dense, begun), (projected, *outs) = refs[:count], refs[count : count + 3], refs[count + 3 :]
    tile, far = pieces[0].shape[0], begun.shape[0]
    for j, piece in enumerate(pieces):
        value = jnp.dot(piece[...], weight[...], preferred_element_type=jnp.float32)
        projected[j * tile : (j + 1) * tile] = value.astype(projected.dtype)
    for k, out in enumerate(outs):
        value = jnp.dot(
            dense[(far + k) * tile : (far + k + 1) * tile, count * tile :],
            projected[...],
            preferred_element_type=jnp.float32,
        )
        out[...] = (begun[k] + value).astype(out.dtype)


def product_kernel(first, second, dense, *outs):
    tile, width = outs[0].shape[0], first.shape[0]
    for p, out in enumerate(outs):
        rows = dense[p * tile : (p + 1) * tile]
        value = jnp.dot(rows[:, :width], first[...], preferred_element_type=jnp.float32)
        value = value + jnp.dot(rows[:, width:], second[...], preferred_element_type=jnp.float32)
        out[...] = value.astype(out.dtype)


def start(pieces, weight, dense, far):
    tile, width = pieces[0].shape
    return pl.pallas_call(
        lambda *refs: start_kernel(len(pieces), *refs),
        out_shape=(
            jax.ShapeDtypeStruct((len(pieces) * tile, width), jnp.bfloat16),
            jax.ShapeDtypeStruct((far, tile, width), jnp.float32),
        ),
        compiler_params=pltpu.CompilerParams(vmem_limit_bytes=limit(dense.size)),
        cost_estimate=pl.CostEstimate(flops=dense.size * width // 2, bytes_accessed=0, transcendentals=0),
    )(*pieces, weight, dense)


def forward(begun, pieces, weight, dense, far):
    first, begun = begun
    tile, width = pieces[0].shape
    params = pltpu.CompilerParams(vmem_limit_bytes=limit(dense.size))
    out = [jax.ShapeDtypeStruct((tile, width), jnp.bfloat16)] * far
    second, *outs = pl.pallas_call(
        lambda *refs: finish_kernel(len(pieces), *refs),
        out_shape=[jax.ShapeDtypeStruct((len(pieces) * tile, width), jnp.bfloat16), *out],
        compiler_params=params,
        cost_estimate=pl.CostEstimate(flops=dense.size * width // 2, bytes_accessed=0, transcendentals=0),
    )(*pieces, weight, dense, begun)
    product = {far + k: value for k, value in enumerate(outs)}
    outs = pl.pallas_call(
        product_kernel,
        out_shape=out,
        compiler_params=params,
        cost_estimate=pl.CostEstimate(flops=dense.size * width, bytes_accessed=0, transcendentals=0),
    )(first, second, dense)
    return {**product, **dict(enumerate(outs))}


def backward_kernel(places, *refs):
    count = len(places)
    pieces, (dense, weight), outs, grads = refs[:count], refs[count : count + 2], refs[count + 2 : -1], refs[-1]
    tile = pieces[0].shape[1]
    half = grads.shape[0] // 2
    for p, piece in zip(places, pieces):
        grads[p * tile : (p + 1) * tile] = piece[0]
        grads[half + p * tile : half + (p + 1) * tile] = piece[1]
    values = [
        lax.dot_general(
            dense[:, j * tile : (j + 1) * tile], grads[...], (((0,), (0,)), ((), ())), preferred_element_type=jnp.float32
        ).astype(outs[0].dtype)
        for j in range(len(outs))
    ]
    for j, out in enumerate(outs):
        if j > len(outs) // 2:
            value = lax.dot_general(values[j], weight[...], (((1,), (1,)), ((), ())), preferred_element_type=jnp.float32)
            out[...] = value.astype(out.dtype)
        else:
            out[...] = values[j]


def backward(places, pieces, dense, weight):
    _, tile, width = pieces[0].shape
    return pl.pallas_call(
        lambda *refs: backward_kernel(places, *refs),
        out_shape=[jax.ShapeDtypeStruct((tile, width), jnp.bfloat16)] * (dense.shape[1] // tile),
        scratch_shapes=[pltpu.VMEM((2 * len(pieces) * tile, width), jnp.bfloat16)],
        compiler_params=pltpu.CompilerParams(vmem_limit_bytes=limit(dense.size)),
        cost_estimate=pl.CostEstimate(flops=2 * dense.size * width, bytes_accessed=0, transcendentals=0),
    )(*pieces, dense, weight)


def shards(features, weight, out_bias, tile_values, tile_cols, tile_counts, cotangent):
    far = lax.axis_size("col") // 2
    near = {"far": (3, 2, 1), "own": (3, 1, 2)} if far == 4 else {"far": range(1, far), "own": range(1, far)}
    rows = range(1, lax.axis_size("row"))
    own = features[0, 0]
    even = [s for s in rows if s % 2 == 0]
    pieces = {s: swap(own, row=s) for s in even}
    pieces[0] = own
    pieces[1] = swap(own, row=1)
    dense = dense_block(tile_cols, tile_counts, tile_values)
    dense, *got = lax.optimization_barrier((dense, *(pieces[s] for s in even)))
    twins = [swap(piece, row=1) for piece in got]
    begun = start([own, *got], weight, dense, far)
    product = forward(begun, [pieces[1], *twins], weight, dense, far)
    half = {}
    for p in (far, 0):
        total = product[p].astype(jnp.float32)
        for s in near["far" if p else "own"]:
            total = total + swap(product[p ^ s], col=s).astype(jnp.float32)
        half[p] = total
    other = swap(half[far].astype(jnp.bfloat16), col=far)
    preact = half[0] + other.astype(jnp.float32) + out_bias
    grads = {0: (cotangent[0, 0].astype(jnp.float32) * silu_slope(preact)[1]).astype(jnp.bfloat16)}
    grads[far] = swap(grads[0], col=far)
    preact, grads[far] = lax.optimization_barrier((preact, grads[far]))
    activated = silu_slope(preact)[0].astype(jnp.bfloat16)
    pair = jnp.stack([grads[0], grads[far]])
    places = [1, 2, 3, 0] if far == 4 else list(range(far))
    messages = [swap(pair, col=p) if p else pair for p in places]
    messages[0], activated = lax.optimization_barrier((messages[0], activated))
    back = backward(places, messages, dense, weight)
    back = dict(zip([0, *even, *(s for s in rows if s % 2)], back))
    spread = back[0].astype(jnp.float32)
    for s in (*even, 1):
        spread = spread + swap(back[s], row=s).astype(jnp.float32)
    ready = jnp.dot(spread.astype(jnp.bfloat16), weight.T, preferred_element_type=jnp.float32)
    ready = lax.optimization_barrier(ready)
    for s in even:
        ready = ready + swap(back[s + 1], row=s + 1).astype(jnp.float32)
    return activated[None, None], ready.astype(jnp.bfloat16)[None, None]


def solution(mesh):
    in_specs = (
        P("col", "row", None, None),
        P(),
        P(),
        P("row", "col", None, None, None, None),
        P("row", "col", None, None),
        P("row", "col", None),
        P("row", "col", None, None),
    )
    out_specs = (P("row", "col", None, None), P("col", "row", None, None))
    return jax.shard_map(shards, mesh=mesh, in_specs=in_specs, out_specs=out_specs, check_vma=False)
```

```python
import jax
import jax.numpy as jnp
from jax import lax
from jax.experimental import pallas as pl
from jax.experimental.pallas import tpu as pltpu
from jax.sharding import PartitionSpec as P

BOTH = ("row", "col")
HBM = pl.BlockSpec(memory_space=pltpu.HBM)


def silu_slope(preact):
    sigmoid_z = jax.nn.sigmoid(preact)
    return (preact * sigmoid_z, sigmoid_z * (1.0 + preact * (1.0 - sigmoid_z)))


def swap(value, row=0, col=0):
    rows, cols = lax.axis_size("row"), lax.axis_size("col")
    pairs = [(r * cols + c, (r ^ row) * cols + (c ^ col)) for r in range(rows) for c in range(cols)]
    return lax.ppermute(value, BOTH, pairs)


def limit(count):
    return 56 * 1024 * 1024 if count * 2 > 6 * 1024 * 1024 else 8 * 1024 * 1024


def dense_kernel(cols_hbm, counts_hbm, tiles_hbm, dense, cols, counts, tiles, sems):
    row_tiles, slots, tile, _ = tiles.shape
    width = dense.shape[1]
    me_row, me_col = lax.axis_index("row"), lax.axis_index("col")
    copies = [
        pltpu.make_async_copy(cols_hbm.at[0, 0], cols, sems.at[0]),
        pltpu.make_async_copy(counts_hbm.at[0], counts, sems.at[1]),
        pltpu.make_async_copy(tiles_hbm.at[0, 0], tiles, sems.at[2]),
    ]
    for copy in copies:
        copy.start()
    dense[...] = jnp.zeros(dense.shape, dense.dtype)
    for copy in copies:
        copy.wait()

    def place(position):
        row_tile = position ^ me_col
        start = pl.multiple_of(position * tile, tile)
        for slot in range(slots):

            @pl.when(slot < counts[0, row_tile])
            def _():
                peer = cols[row_tile, slot] ^ me_row
                column = pl.multiple_of((peer // 2 + peer % 2 * (width // tile // 2)) * tile, tile)
                dense[pl.ds(start, tile), pl.ds(column, tile)] = tiles[row_tile, slot]

    if row_tiles <= 8:
        for position in range(row_tiles):
            place(position)
    else:
        pl.loop(0, row_tiles)(place)


def dense_block(tile_cols, tile_counts, tile_values):
    row_tiles, slots, tile, _ = tile_values.shape[2:]
    height, width = row_tiles * tile, lax.axis_size("row") * tile
    kind = tile_values.dtype
    return pl.pallas_call(
        dense_kernel,
        in_specs=[HBM] * 3,
        out_shape=jax.ShapeDtypeStruct((height, width), kind),
        scratch_shapes=[
            pltpu.SMEM((row_tiles, slots), jnp.int32),
            pltpu.SMEM((1, row_tiles), jnp.int32),
            pltpu.VMEM((row_tiles, slots, tile, tile), kind),
            pltpu.SemaphoreType.DMA((3,)),
        ],
        compiler_params=pltpu.CompilerParams(vmem_limit_bytes=limit(height * width)),
        cost_estimate=pl.CostEstimate(flops=0, bytes_accessed=tile_values.size * 2, transcendentals=0),
    )(tile_cols, tile_counts, tile_values)


def start_kernel(count, *refs):
    pieces, (weight, dense), (projected, begun) = refs[:count], refs[count : count + 2], refs[count + 2 :]
    tile, far = pieces[0].shape[0], begun.shape[0]
    for j, piece in enumerate(pieces):
        value = jnp.dot(piece[...], weight[...], preferred_element_type=jnp.float32)
        projected[j * tile : (j + 1) * tile] = value.astype(projected.dtype)
    for k in range(far):
        begun[k] = jnp.dot(
            dense[(far + k) * tile : (far + k + 1) * tile, : count * tile],
            projected[...],
            preferred_element_type=jnp.float32,
        )


def finish_kernel(count, *refs):
    pieces, (weight, dense, begun), (projected, *outs) = refs[:count], refs[count : count + 3], refs[count + 3 :]
    tile, far = pieces[0].shape[0], begun.shape[0]
    for j, piece in enumerate(pieces):
        value = jnp.dot(piece[...], weight[...], preferred_element_type=jnp.float32)
        projected[j * tile : (j + 1) * tile] = value.astype(projected.dtype)
    for k, out in enumerate(outs):
        value = jnp.dot(
            dense[(far + k) * tile : (far + k + 1) * tile, count * tile :],
            projected[...],
            preferred_element_type=jnp.float32,
        )
        out[...] = (begun[k] + value).astype(out.dtype)


def product_kernel(first, second, dense, *outs):
    tile, width = outs[0].shape[0], first.shape[0]
    for p, out in enumerate(outs):
        rows = dense[p * tile : (p + 1) * tile]
        value = jnp.dot(rows[:, :width], first[...], preferred_element_type=jnp.float32)
        value = value + jnp.dot(rows[:, width:], second[...], preferred_element_type=jnp.float32)
        out[...] = value.astype(out.dtype)


def start(pieces, weight, dense, far):
    tile, width = pieces[0].shape
    return pl.pallas_call(
        lambda *refs: start_kernel(len(pieces), *refs),
        out_shape=(
            jax.ShapeDtypeStruct((len(pieces) * tile, width), jnp.bfloat16),
            jax.ShapeDtypeStruct((far, tile, width), jnp.float32),
        ),
        compiler_params=pltpu.CompilerParams(vmem_limit_bytes=limit(dense.size)),
        cost_estimate=pl.CostEstimate(flops=dense.size * width // 2, bytes_accessed=0, transcendentals=0),
    )(*pieces, weight, dense)


def forward(begun, pieces, weight, dense, far):
    first, begun = begun
    tile, width = pieces[0].shape
    params = pltpu.CompilerParams(vmem_limit_bytes=limit(dense.size))
    out = [jax.ShapeDtypeStruct((tile, width), jnp.bfloat16)] * far
    second, *outs = pl.pallas_call(
        lambda *refs: finish_kernel(len(pieces), *refs),
        out_shape=[jax.ShapeDtypeStruct((len(pieces) * tile, width), jnp.bfloat16), *out],
        compiler_params=params,
        cost_estimate=pl.CostEstimate(flops=dense.size * width // 2, bytes_accessed=0, transcendentals=0),
    )(*pieces, weight, dense, begun)
    product = {far + k: value for k, value in enumerate(outs)}
    outs = pl.pallas_call(
        product_kernel,
        out_shape=out,
        compiler_params=params,
        cost_estimate=pl.CostEstimate(flops=dense.size * width, bytes_accessed=0, transcendentals=0),
    )(first, second, dense)
    return {**product, **dict(enumerate(outs))}


def backward_kernel(places, *refs):
    count = len(places)
    pieces, (dense, weight), outs, grads = refs[:count], refs[count : count + 2], refs[count + 2 : -1], refs[-1]
    tile = pieces[0].shape[1]
    half = grads.shape[0] // 2
    for p, piece in zip(places, pieces):
        grads[p * tile : (p + 1) * tile] = piece[0]
        grads[half + p * tile : half + (p + 1) * tile] = piece[1]
    for j, out in enumerate(outs):
        value = lax.dot_general(
            dense[:, j * tile : (j + 1) * tile], grads[...], (((0,), (0,)), ((), ())), preferred_element_type=jnp.float32
        )
        if j > len(outs) // 2:
            value = lax.dot_general(
                value.astype(out.dtype), weight[...], (((1,), (1,)), ((), ())), preferred_element_type=jnp.float32
            )
        out[...] = value.astype(out.dtype)


def backward(places, pieces, dense, weight):
    _, tile, width = pieces[0].shape
    return pl.pallas_call(
        lambda *refs: backward_kernel(places, *refs),
        out_shape=[jax.ShapeDtypeStruct((tile, width), jnp.bfloat16)] * (dense.shape[1] // tile),
        scratch_shapes=[pltpu.VMEM((2 * len(pieces) * tile, width), jnp.bfloat16)],
        compiler_params=pltpu.CompilerParams(vmem_limit_bytes=limit(dense.size)),
        cost_estimate=pl.CostEstimate(flops=2 * dense.size * width, bytes_accessed=0, transcendentals=0),
    )(*pieces, dense, weight)


def shards(features, weight, out_bias, tile_values, tile_cols, tile_counts, cotangent):
    far = lax.axis_size("col") // 2
    near = {"far": (3, 2, 1), "own": (3, 1, 2)} if far == 4 else {"far": range(1, far), "own": range(1, far)}
    rows = range(1, lax.axis_size("row"))
    own = features[0, 0]
    even = [s for s in rows if s % 2 == 0]
    pieces = {s: swap(own, row=s) for s in even}
    pieces[0] = own
    pieces[1] = swap(own, row=1)
    dense = dense_block(tile_cols, tile_counts, tile_values)
    dense, *got = lax.optimization_barrier((dense, *(pieces[s] for s in even)))
    twins = [swap(piece, row=1) for piece in got]
    begun = start([own, *got], weight, dense, far)
    product = forward(begun, [pieces[1], *twins], weight, dense, far)
    half = {}
    for p in (far, 0):
        total = product[p].astype(jnp.float32)
        for s in near["far" if p else "own"]:
            total = total + swap(product[p ^ s], col=s).astype(jnp.float32)
        half[p] = total
    other = swap(half[far].astype(jnp.bfloat16), col=far)
    preact = half[0] + other.astype(jnp.float32) + out_bias
    grads = {0: (cotangent[0, 0].astype(jnp.float32) * silu_slope(preact)[1]).astype(jnp.bfloat16)}
    grads[far] = swap(grads[0], col=far)
    preact, grads[far] = lax.optimization_barrier((preact, grads[far]))
    pair = jnp.stack([grads[0], grads[far]])
    places = [1, 2, 3, 0] if far == 4 else list(range(far))
    back = backward(places, [swap(pair, col=p) if p else pair for p in places], dense, weight)
    back = dict(zip([0, *even, *(s for s in rows if s % 2)], back))
    spread = back[0].astype(jnp.float32)
    for s in (*even, 1):
        got = swap(back[s], row=s)
        if s == even[-1]:
            preact, got = lax.optimization_barrier((preact, got))
        spread = spread + got.astype(jnp.float32)
    activated = silu_slope(preact)[0].astype(jnp.bfloat16)
    ready = jnp.dot(spread.astype(jnp.bfloat16), weight.T, preferred_element_type=jnp.float32)
    ready = lax.optimization_barrier(ready)
    for s in even:
        ready = ready + swap(back[s + 1], row=s + 1).astype(jnp.float32)
    return activated[None, None], ready.astype(jnp.bfloat16)[None, None]


def solution(mesh):
    in_specs = (
        P("col", "row", None, None),
        P(),
        P(),
        P("row", "col", None, None, None, None),
        P("row", "col", None, None),
        P("row", "col", None),
        P("row", "col", None, None),
    )
    out_specs = (P("row", "col", None, None), P("col", "row", None, None))
    return jax.shard_map(shards, mesh=mesh, in_specs=in_specs, out_specs=out_specs, check_vma=False)
```
